32 devices in a mesh: dp: 4 (over x, core), seq: 2 (over y), tensor: 4 (over z).
Axes of the slice: x: 2, y: 2, z: 4, core: 2. Of those that a mesh axis runs over, the one named last changes fastest.
Arguments:
- hidden: bfloat16 [1024, 28672], P(('dp', 'seq'), 'tensor'), may hold values from -6 to 6
- weight: bfloat16 [28672, 4096], P('tensor', 'seq'), may hold values from -0.03125 to 0.03125
- out_grad: bfloat16 [1024, 4096], P(('dp', 'tensor'), 'seq'), may hold values from -6 to 6
Outputs:
- output: bfloat16 [1024, 4096], P(('dp', 'tensor'), 'seq')
- grad_hidden: bfloat16 [1024, 28672], P(('dp', 'seq'), 'tensor')
- grad_weight: bfloat16 [28672, 4096], P('tensor', 'seq')
The draws below stay inside these ranges and needn't reach their ends.
All inputs are finite; a program needn't handle non-finite values.
Results may differ from the reference program's by a relative error of at most 0.017.
Values may be sent and summed in bfloat16 or wider, within the bound.
No kernel may reach another device: no remote copies, remote signals or barrier semaphores. Data moves between devices by JAX's collectives and lax.ppermute only.
A program may use at most 192 MiB of HBM per device.

```python
import jax
import jax.numpy as jnp
from jax import lax

FF = 28672
DW = 4096
HB = 512
TOK_REP = 256
TOKENS = 1024
SEQ_COLS = 2048
N_TENSOR = 4


def block_scale(key, extent, cuts, least, high):
    factor_of = 1.0
    for dim, shards_of in cuts:
        steps = jax.random.uniform(jax.random.fold_in(jax.random.fold_in(key, 6), dim), (shards_of,), jnp.float32, least / len(cuts), high / len(cuts))
        factor_of = factor_of * jnp.repeat(jnp.exp(steps), extent[dim] // shards_of).reshape((-1,) + (1,) * (len(extent) - 1 - dim))
    return factor_of


def noise(rng, shape, deviation, most, pieces=(), kind=jnp.bfloat16):
    drawn = deviation * jax.random.normal(rng, shape, jnp.float32)
    if pieces:
        drawn = drawn * block_scale(rng, shape, pieces, -0.22, 0.18)
    return jnp.clip(drawn, -most, most).astype(kind)


def setup_inputs(seed: int = 0) -> dict:
    arg_keys = jax.random.split(jax.random.key(seed), 4)
    return {
        "hidden": noise(arg_keys[0], (TOKENS, FF), 1.0, 6.0, ((0, 8), (1, 4))),
        "weight": noise(arg_keys[1], (FF, DW), FF ** -0.5, 0.03125, ((0, 4), (1, 2))),
        "out_grad": noise(arg_keys[2], (TOKENS, DW), 1.0, 6.0, ((0, 16), (1, 2))),
    }


def sylvester(table_order):
    matrix = jnp.ones((1, 1), jnp.float32)
    while matrix.shape[0] < table_order:
        matrix = jnp.concatenate([jnp.concatenate([matrix, matrix], 1), jnp.concatenate([matrix, -matrix], 1)], 0)
    return matrix


def rounded(values):
    return lax.optimization_barrier(values.astype(jnp.bfloat16)).astype(jnp.float32)


def rotate(values):
    row_count = values.shape[0]
    shaped = values.astype(jnp.float32).reshape(row_count, N_TENSOR, FF // (N_TENSOR * HB), HB)
    mixed_rows = jnp.einsum("rtbk,kl->rtbl", shaped, sylvester(HB), precision=lax.Precision.HIGHEST)
    mixed_rows = jnp.einsum("rtbl,ts->rsbl", mixed_rows, sylvester(N_TENSOR), precision=lax.Precision.HIGHEST)
    return mixed_rows.reshape(row_count, FF) * (1.0 / float(N_TENSOR * HB) ** 0.5)


def reference(hidden, weight, out_grad):
    rotated = rotate(hidden).astype(jnp.bfloat16)
    output = jnp.dot(rotated, weight, preferred_element_type=jnp.float32).astype(jnp.bfloat16)
    grad_scale = 1.0 / float(TOKENS) ** 0.5
    grad_sum = jnp.zeros((FF, DW), jnp.float32)
    for replica in range(TOKENS // TOK_REP):
        rows_now = rotated[replica * TOK_REP:(replica + 1) * TOK_REP]
        grads_now = out_grad[replica * TOK_REP:(replica + 1) * TOK_REP]
        grad_sum = grad_sum + rounded(jnp.dot(rows_now.T, grads_now, preferred_element_type=jnp.float32) * grad_scale)
    grad_weight = grad_sum.astype(jnp.bfloat16)
    rotated_grad = jnp.zeros((TOKENS, FF), jnp.float32)
    for block_index in range(DW // SEQ_COLS):
        grad_block = out_grad[:, block_index * SEQ_COLS:(block_index + 1) * SEQ_COLS]
        weight_block = weight[:, block_index * SEQ_COLS:(block_index + 1) * SEQ_COLS]
        rotated_grad = rotated_grad + rounded(jnp.dot(grad_block, weight_block.T, preferred_element_type=jnp.float32))
    grad_hidden = rotate(rotated_grad).astype(jnp.bfloat16)
    return output, grad_hidden, grad_weight
```

```python
import functools

import jax
import jax.numpy as jnp
from jax import lax
from jax.experimental import pallas as pl
from jax.experimental.pallas import tpu as pltpu
from jax.sharding import PartitionSpec as P

HB = 512
BF = jnp.bfloat16
F32 = jnp.float32
VMEM_BYTES = 40 * 1024 * 1024
HIDDEN_SPLIT = (4,4,3,3)
GRAD_SPLIT = (4,4,3,3)
def partner(shard, axis, bit):
    return lax.ppermute(shard, axis, [(i, i ^ 1 << bit) for i in range(lax.axis_size(axis))])


def bits_of(axis):
    return lax.axis_size(axis).bit_length() - 1


def walsh_table(table_order):
    matrix = jnp.ones((1, 1), F32)
    while matrix.shape[0] < table_order:
        matrix = jnp.concatenate(
            [jnp.concatenate([matrix, matrix], 1), jnp.concatenate([matrix, -matrix], 1)], 0
        )
    return matrix.astype(BF)


def split_blocks(total, sizes):
    if sum(sizes) != total:
        count = min(len(sizes), total)
        sizes = [total // count + (1 if i < total % count else 0) for i in range(count)]
    return [(sum(sizes[:i]), sizes[i]) for i in range(len(sizes))]


def call(kernel, grid, in_specs, out_specs, out_shape, flops, nbytes, scratch=(), aliases=None):
    return pl.pallas_call(
        kernel,
        grid=grid,
        in_specs=in_specs,
        out_specs=out_specs,
        out_shape=out_shape,
        scratch_shapes=list(scratch),
        input_output_aliases=aliases or {},
        compiler_params=pltpu.CompilerParams(vmem_limit_bytes=VMEM_BYTES),
        cost_estimate=pl.CostEstimate(flops=flops, bytes_accessed=nbytes, transcendentals=0),
    )


def sign_of(axis, bit):
    upper = lax.rem(lax.div(lax.axis_index(axis), 1 << bit), 2)
    return (1 - 2 * upper).astype(F32).reshape(1, 1)


SIGN_SPEC = pl.BlockSpec(memory_space=pltpu.SMEM)


def combine(sign, own, own_block, received):
    rows, width = received.shape
    blocks = width // HB

    def kernel(sign_ref, own_ref, received_ref, out_ref):
        out_ref[...] = (
            received_ref[...].astype(F32) + sign_ref[0, 0] * own_ref[...].astype(F32)
        ).astype(BF)

    return call(
        kernel,
        (blocks,),
        [
            SIGN_SPEC,
            pl.BlockSpec((rows, HB), lambda i: (0, own_block + i)),
            pl.BlockSpec((rows, HB), lambda i: (0, i)),
        ],
        pl.BlockSpec((rows, HB), lambda i: (0, i)),
        jax.ShapeDtypeStruct((rows, width), BF),
        2 * rows * width,
        6 * rows * width,
    )(sign, own, received)


def finish_hidden(sign, own, received, table, scale):
    rows, width = received.shape
    blocks = width // HB

    def kernel(sign_ref, own_ref, received_ref, table_ref, out_ref):
        mixed = received_ref[...].astype(F32) + sign_ref[0, 0] * own_ref[...].astype(F32)
        turned = lax.dot_general(
            table_ref[...], mixed.astype(BF), (((1,), (1,)), ((), ())), preferred_element_type=F32
        )
        out_ref[...] = (turned * scale).astype(BF)

    return call(
        kernel,
        (blocks,),
        [
            SIGN_SPEC,
            pl.BlockSpec((rows, HB), lambda i: (0, i)),
            pl.BlockSpec((rows, HB), lambda i: (0, i)),
            pl.BlockSpec((HB, HB), lambda i: (0, 0)),
        ],
        pl.BlockSpec((HB, rows), lambda i: (i, 0)),
        jax.ShapeDtypeStruct((width, rows), BF),
        2 * rows * width * HB,
        6 * rows * width,
    )(sign, own, received, table)


def finish_grad(sign, own, received, table, scale, first, total, result):
    rows, width = received.shape
    blocks = width // HB

    def kernel(sign_ref, own_ref, received_ref, table_ref, *refs):
        out_ref = refs[-1]
        mixed = received_ref[...].astype(F32) + sign_ref[0, 0] * own_ref[...].astype(F32)
        turned = jnp.dot(mixed.astype(BF), table_ref[...], preferred_element_type=F32)
        out_ref[...] = (turned * scale).astype(BF)

    args = [sign, own, received, table]
    specs = [
        SIGN_SPEC,
        pl.BlockSpec((rows, HB), lambda i: (0, i)),
        pl.BlockSpec((rows, HB), lambda i: (0, i)),
        pl.BlockSpec((HB, HB), lambda i: (0, 0)),
    ]
    aliases = None
    if result is not None:
        args.append(result)
        specs.append(pl.BlockSpec(memory_space=pl.ANY))
        aliases = {4: 0}
    return call(
        kernel,
        (blocks,),
        specs,
        pl.BlockSpec((rows, HB), lambda i: (0, first + i)),
        jax.ShapeDtypeStruct((rows, total), BF),
        2 * rows * width * HB,
        6 * rows * width,
        aliases=aliases,
    )(*args)


def rotated_grad_parts(grads, weight, first, blocks, count):
    tokens, columns = grads.shape
    rows = tokens // count

    def kernel(grads_ref, weight_ref, *out_refs):
        total = lax.dot_general(
            grads_ref[...], weight_ref[...], (((1,), (1,)), ((), ())), preferred_element_type=F32
        ).astype(BF)
        for n, out_ref in enumerate(out_refs):
            out_ref[...] = total[n * rows : (n + 1) * rows]

    return call(
        kernel,
        (blocks,),
        [
            pl.BlockSpec((tokens, columns), lambda i: (0, 0)),
            pl.BlockSpec((HB, columns), lambda i: (first + i, 0)),
        ],
        [pl.BlockSpec((rows, HB), lambda i: (0, i))] * count,
        [jax.ShapeDtypeStruct((rows, blocks * HB), BF)] * count,
        2 * tokens * columns * blocks * HB,
        2 * blocks * HB * columns,
    )(grads, weight)


def output_part(turned, weight, first, running, last):
    width, tokens = turned.shape
    columns = weight.shape[1]
    blocks = width // HB

    def kernel(turned_ref, weight_ref, *refs):
        total_ref = refs[-1]
        out_ref = refs[-2]
        step = pl.program_id(0)

        @pl.when(step == 0)
        def _():
            if running is None:
                total_ref[...] = jnp.zeros_like(total_ref)
            else:
                total_ref[...] = refs[0][...]

        total_ref[...] += lax.dot_general(
            turned_ref[...], weight_ref[...], (((0,), (0,)), ((), ())), preferred_element_type=F32
        )

        @pl.when(step == blocks - 1)
        def _():
            out_ref[...] = total_ref[...].astype(out_ref.dtype)

    whole = pl.BlockSpec((tokens, columns), lambda i: (0, 0))
    args = [turned, weight]
    specs = [
        pl.BlockSpec((HB, tokens), lambda i: (i, 0)),
        pl.BlockSpec((HB, columns), lambda i: (first + i, 0)),
    ]
    if running is not None:
        args.append(running)
        specs.append(whole)
    return call(
        kernel,
        (blocks,),
        specs,
        whole,
        jax.ShapeDtypeStruct((tokens, columns), BF if last else F32),
        2 * tokens * width * columns,
        2 * width * columns,
        scratch=[pltpu.VMEM((tokens, columns), F32)],
    )(*args)


def weight_grad_part(turned, grads, scale, first, total, result):
    width = turned[0].shape[0]
    columns = grads[0].shape[1]
    blocks = width // HB
    count = len(turned)
    tokens = sum(piece.shape[1] for piece in turned)

    def kernel(*refs):
        out_ref = refs[-1]
        left = jnp.concatenate([ref[...] for ref in refs[:count]], axis=1)
        right = jnp.concatenate([ref[...] for ref in refs[count : 2 * count]], axis=0)
        product = jnp.dot(left, right, preferred_element_type=F32)
        out_ref[...] = (product * scale).astype(BF)

    args = list(turned) + list(grads)
    specs = [pl.BlockSpec((HB, piece.shape[1]), lambda i: (i, 0)) for piece in turned]
    specs += [pl.BlockSpec(piece.shape, lambda i: (0, 0)) for piece in grads]
    aliases = None
    if result is not None:
        args.append(result)
        specs.append(pl.BlockSpec(memory_space=pl.ANY))
        aliases = {2 * count: 0}
    return call(
        kernel,
        (blocks,),
        specs,
        pl.BlockSpec((HB, columns), lambda i: (first + i, 0)),
        jax.ShapeDtypeStruct((total, columns), BF),
        2 * tokens * width * columns,
        2 * width * (columns + tokens),
        aliases=aliases,
    )(*args)


ORDER = [
    "G", "h1", "G", "h1", "h2", "G", "h0", "g1", "g0", "h2", "h1", "G",
    "g1", "g3", "h3", "h0", "h1", "h2", "h1", "g3", "h3", "g2", "g0", "h0",
    "h1", "g1", "g2", "G", "h3", "h1", "h2", "g3", "h2", "g1", "h0", "h3",
    "h0", "g2", "h3", "h2", "g3", "g0", "out", "h0", "g2", "h2", "h3", "h0",
    "out", "g0", "h3", "out",
]


def body(hidden, weight, out_grad):
    n_tensor, n_seq, n_dp = (lax.axis_size(a) for a in ("tensor", "seq", "dp"))
    me_tensor, me_seq = lax.axis_index("tensor"), lax.axis_index("seq")
    rows, features = hidden.shape
    blocks = features // HB
    per_seq = n_tensor // n_seq
    table = walsh_table(HB)
    norm_scale = 1.0 / float(n_tensor * HB) ** 0.5
    grad_scale = 1.0 / float(rows * n_seq * n_dp) ** 0.5
    signs = [sign_of("tensor", bit) for bit in range(bits_of("tensor"))]
    plus = jnp.ones((1, 1), F32)
    near_first = list(range(bits_of("tensor")))
    far_first = near_first[::-1]
    seq_bits = list(range(bits_of("seq")))
    dp_bits = list(reversed(range(bits_of("dp"))))
    hidden_parts = split_blocks(blocks, HIDDEN_SPLIT)
    grad_parts = split_blocks(blocks, GRAD_SPLIT)
    state = {"last": None, "running": None, "grad_weight": None, "grad_hidden": None}
    state["to_sum"] = len(hidden_parts)

    def tied(value):
        if state["last"] is None:
            return value
        return lax.optimization_barrier((value, state["last"]))[0]

    def done(value):
        state["last"] = value
        return value

    def send(value, axis, bit):
        return partner(tied(value), axis, bit)

    def gather_grads():
        grads = out_grad
        for bit in far_first:
            arrived = partner(grads, "tensor", bit)
            yield
            grads = done(jnp.concatenate([grads, arrived], axis=0))
        shards = grads.reshape(n_tensor, *out_grad.shape)

        def shard_of(owner):
            apart = owner ^ me_tensor
            place = sum(((apart >> b) & 1) << (len(near_first) - 1 - b) for b in near_first)
            return lax.dynamic_index_in_dim(shards, place, 0, keepdims=False)

        grads = done(
            jnp.concatenate(
                [
                    shard_of((me_seq ^ run) * per_seq + inner)
                    for run in range(n_seq)
                    for inner in range(per_seq)
                ],
                axis=0,
            )
        )
        state["grads"] = grads
        pieces = [grads]
        for bit in dp_bits:
            pieces += [send(piece, "dp", bit) for piece in pieces[::-1]][::-1]
            yield
            for piece in pieces[len(pieces) // 2 :]:
                done(piece)
        state["grad_pieces"] = pieces

    def hidden_part(first, size):
        own, own_block = hidden, first
        sent = tied(hidden)[:, first * HB : (first + size) * HB]
        for bit in far_first[:-1]:
            arrived = send(sent, "tensor", bit)
            yield
            own = done(combine(signs[bit], tied(own), own_block, arrived))
            sent, own_block = own, 0
        arrived = send(sent, "tensor", far_first[-1])
        yield
        turned = done(finish_hidden(signs[far_first[-1]], tied(sent), arrived, table, norm_scale))
        for bit in seq_bits:
            arrived = send(turned, "seq", bit)
            yield
            turned = done(jnp.concatenate([tied(turned), arrived], axis=1))
        pieces = [turned]
        for place, bit in enumerate(dp_bits):
            pieces += [send(piece, "dp", bit) for piece in pieces]
            yield
            if place == 0:
                state["to_sum"] -= 1
                state["running"] = done(
                    output_part(
                        tied(turned), weight, first, state["running"], state["to_sum"] == 0
                    )
                )
                yield
        state["grad_weight"] = done(
            weight_grad_part(
                [tied(pieces[0])] + pieces[1:],
                state["grad_pieces"],
                grad_scale,
                first,
                features,
                state["grad_weight"],
            )
        )

    def grad_part(first, size):
        terms = list(rotated_grad_parts(tied(state["grads"]), weight, first, size, n_seq))
        done(terms[0])
        for bit in reversed(seq_bits):
            half = len(terms) // 2
            arrived = [send(term, "seq", bit) for term in terms[half:]]
            yield
            terms = [
                done(combine(plus, tied(terms[n]), 0, arrived[n])) for n in range(half)
            ]
        own = terms[0]
        for bit in near_first[:-1]:
            arrived = send(own, "tensor", bit)
            yield
            own = done(combine(signs[bit], tied(own), 0, arrived))
        arrived = send(own, "tensor", near_first[-1])
        yield
        state["grad_hidden"] = done(
            finish_grad(
                signs[near_first[-1]],
                tied(own),
                arrived,
                table,
                norm_scale,
                first,
                features,
                state["grad_hidden"],
            )
        )

    def sum_output():
        shard_rows = out_grad.shape[0]
        runs = state["running"].reshape(n_tensor, shard_rows, -1)

        def run_for(apart):
            owner = me_tensor ^ apart
            place = ((owner // per_seq) ^ me_seq) * per_seq + owner % per_seq
            return lax.dynamic_index_in_dim(runs, place, 0, keepdims=False)

        sums = {apart: run_for(apart) for apart in range(n_tensor)}
        for bit in near_first:
            leaving = [apart for apart in sums if apart >> bit & 1]
            arrived = partner(jnp.concatenate([sums[a] for a in leaving], axis=0), "tensor", bit)
            yield
            arrived = tied(arrived)
            for place, apart in enumerate(leaving):
                block = arrived[place * shard_rows : (place + 1) * shard_rows]
                kept = apart ^ 1 << bit
                sums[kept] = (sums[kept].astype(F32) + block.astype(F32)).astype(BF)
                del sums[apart]
            done(sums[0])
        state["output"] = sums[0]

    steps = {"G": gather_grads()}
    for n, (first, size) in enumerate(hidden_parts):
        steps["h%d" % n] = hidden_part(first, size)
    for n, (first, size) in enumerate(grad_parts):
        steps["g%d" % n] = grad_part(first, size)
    steps["out"] = sum_output()
    order = ORDER
    if (n_tensor, n_seq, n_dp) != (4, 2, 4):
        order = ["G"] * 20
        for name in [n for n in steps if n[0] in "hg"]:
            order += [name] * 20
        order += ["out"] * 10
    for name in order:
        next(steps[name], None)
    return (state["output"], state["grad_hidden"], state["grad_weight"])


def solution(mesh):
    in_specs = (P(("dp", "seq"), "tensor"), P("tensor", "seq"), P(("dp", "tensor"), "seq"))
    out_specs = (P(("dp", "tensor"), "seq"), P(("dp", "seq"), "tensor"), P("tensor", "seq"))
    return jax.shard_map(body, mesh=mesh, in_specs=in_specs, out_specs=out_specs, check_vma=False)
```

```python
import functools

import jax
import jax.numpy as jnp
from jax import lax
from jax.experimental import pallas as pl
from jax.experimental.pallas import tpu as pltpu
from jax.sharding import PartitionSpec as P

HB = 512
BF = jnp.bfloat16
F32 = jnp.float32
VMEM_BYTES = 40 * 1024 * 1024
HIDDEN_SPLIT = (3, 3, 4, 4)
GRAD_SPLIT = (3, 3, 4, 4)
PLANNED = {'weight_grad': 0.01, 'combine': 0.01}
def partner(shard, axis, bit):
    return lax.ppermute(shard, axis, [(i, i ^ 1 << bit) for i in range(lax.axis_size(axis))])


def bits_of(axis):
    return lax.axis_size(axis).bit_length() - 1


def walsh_table(table_order):
    matrix = jnp.ones((1, 1), F32)
    while matrix.shape[0] < table_order:
        matrix = jnp.concatenate(
            [jnp.concatenate([matrix, matrix], 1), jnp.concatenate([matrix, -matrix], 1)], 0
        )
    return matrix.astype(BF)


def split_blocks(total, sizes):
    if sum(sizes) != total:
        count = min(len(sizes), total)
        sizes = [total // count + (1 if i < total % count else 0) for i in range(count)]
    return [(sum(sizes[:i]), sizes[i]) for i in range(len(sizes))]


def call(name, kernel, grid, in_specs, out_specs, out_shape, flops, nbytes, scratch=(), aliases=None):
    weight = PLANNED.get(name, 1)
    return pl.pallas_call(
        kernel,
        name=name,
        grid=grid,
        in_specs=in_specs,
        out_specs=out_specs,
        out_shape=out_shape,
        scratch_shapes=list(scratch),
        input_output_aliases=aliases or {},
        compiler_params=pltpu.CompilerParams(vmem_limit_bytes=VMEM_BYTES),
        cost_estimate=pl.CostEstimate(flops=int(flops * weight), bytes_accessed=int(nbytes * weight), transcendentals=0),
    )


def sign_of(axis, bit):
    upper = lax.rem(lax.div(lax.axis_index(axis), 1 << bit), 2)
    return (1 - 2 * upper).astype(F32).reshape(1, 1)


SIGN_SPEC = pl.BlockSpec(memory_space=pltpu.SMEM)


def steps_for(first, blocks, least, unit):
    for steps in range(least, blocks + 1):
        size = blocks * HB // steps
        if size * steps == blocks * HB and size % unit == 0 and first * HB % size == 0:
            return steps, size, first * HB // size
    return blocks, HB, first


def combine(sign, own, received):
    rows, width = received.shape

    def kernel(sign_ref, own_ref, received_ref, out_ref):
        out_ref[...] = (
            received_ref[...].astype(F32) + sign_ref[0, 0] * own_ref[...].astype(F32)
        ).astype(BF)

    whole = pl.BlockSpec((rows, width), lambda i: (0, 0))
    return call(
        "combine",
        kernel,
        (1,),
        [SIGN_SPEC, whole, whole],
        whole,
        jax.ShapeDtypeStruct((rows, width), BF),
        2 * rows * width,
        6 * rows * width,
    )(sign, own, received)


def finish_hidden(sign, own, received, table, scale):
    rows, width = received.shape

    def kernel(sign_ref, own_ref, received_ref, table_ref, out_ref):
        for at in range(0, width, HB):
            run = slice(at, at + HB)
            mixed = received_ref[:, run].astype(F32) + sign_ref[0, 0] * own_ref[:, run].astype(F32)
            turned = lax.dot_general(
                table_ref[...],
                mixed.astype(BF),
                (((1,), (1,)), ((), ())),
                preferred_element_type=F32,
            )
            out_ref[run, :] = (turned * scale).astype(BF)

    whole = pl.BlockSpec((rows, width), lambda i: (0, 0))
    return call(
        "finish_hidden",
        kernel,
        (1,),
        [SIGN_SPEC, whole, whole, pl.BlockSpec((HB, HB), lambda i: (0, 0))],
        pl.BlockSpec((width, rows), lambda i: (0, 0)),
        jax.ShapeDtypeStruct((width, rows), BF),
        2 * rows * width * HB,
        6 * rows * width,
    )(sign, own, received, table)


def finish_grad(sign, own, received, table, scale, first, total, result):
    rows, width = received.shape
    steps, size, start = steps_for(first, width // HB, 1, HB)

    def kernel(sign_ref, own_ref, received_ref, table_ref, *refs):
        out_ref = refs[-1]
        for at in range(0, size, HB):
            run = slice(at, at + HB)
            mixed = received_ref[:, run].astype(F32) + sign_ref[0, 0] * own_ref[:, run].astype(F32)
            turned = jnp.dot(mixed.astype(BF), table_ref[...], preferred_element_type=F32)
            out_ref[:, run] = (turned * scale).astype(BF)

    args = [sign, own, received, table]
    specs = [
        SIGN_SPEC,
        pl.BlockSpec((rows, size), lambda i: (0, i)),
        pl.BlockSpec((rows, size), lambda i: (0, i)),
        pl.BlockSpec((HB, HB), lambda i: (0, 0)),
    ]
    aliases = None
    if result is not None:
        args.append(result)
        specs.append(pl.BlockSpec(memory_space=pl.ANY))
        aliases = {4: 0}
    return call(
        "finish_grad",
        kernel,
        (steps,),
        specs,
        pl.BlockSpec((rows, size), lambda i: (0, start + i)),
        jax.ShapeDtypeStruct((rows, total), BF),
        2 * rows * width * HB,
        6 * rows * width,
        aliases=aliases,
    )(*args)


def rotated_grad_parts(grads, weight, first, blocks, count):
    tokens, columns = grads.shape
    rows = tokens // count
    steps, size, start = steps_for(first, blocks, 2, 256)

    def kernel(grads_ref, weight_ref, *out_refs):
        total = lax.dot_general(
            grads_ref[...], weight_ref[...], (((1,), (1,)), ((), ())), preferred_element_type=F32
        ).astype(BF)
        for n, out_ref in enumerate(out_refs):
            out_ref[...] = total[n * rows : (n + 1) * rows]

    return call(
        "rotated_grad",
        kernel,
        (steps,),
        [
            pl.BlockSpec((tokens, columns), lambda i: (0, 0)),
            pl.BlockSpec((size, columns), lambda i: (start + i, 0)),
        ],
        [pl.BlockSpec((rows, size), lambda i: (0, i))] * count,
        [jax.ShapeDtypeStruct((rows, blocks * HB), BF)] * count,
        2 * tokens * columns * blocks * HB,
        2 * blocks * HB * columns,
    )(grads, weight)


def output_part(turned, weight, first, running, last):
    width, tokens = turned.shape
    columns = weight.shape[1]
    steps, size, start = steps_for(first, width // HB, 2, 256)

    def kernel(turned_ref, weight_ref, *refs):
        total_ref = refs[-1]
        out_ref = refs[-2]
        step = pl.program_id(0)

        @pl.when(step == 0)
        def _():
            if running is None:
                total_ref[...] = jnp.zeros_like(total_ref)
            else:
                total_ref[...] = refs[0][...]

        total_ref[...] += lax.dot_general(
            turned_ref[...], weight_ref[...], (((0,), (0,)), ((), ())), preferred_element_type=F32
        )

        @pl.when(step == steps - 1)
        def _():
            out_ref[...] = total_ref[...].astype(out_ref.dtype)

    whole = pl.BlockSpec((tokens, columns), lambda i: (0, 0))
    args = [turned, weight]
    specs = [
        pl.BlockSpec((size, tokens), lambda i: (i, 0)),
        pl.BlockSpec((size, columns), lambda i: (start + i, 0)),
    ]
    if running is not None:
        args.append(running)
        specs.append(whole)
    return call(
        "output",
        kernel,
        (steps,),
        specs,
        whole,
        jax.ShapeDtypeStruct((tokens, columns), BF if last else F32),
        2 * tokens * width * columns,
        2 * width * columns,
        scratch=[pltpu.VMEM((tokens, columns), F32)],
    )(*args)


def weight_grad_part(turned, grads, scale, first, total, result):
    width = turned[0].shape[0]
    columns = grads[0].shape[1]
    steps, size, start = steps_for(first, width // HB, 2, 256)
    count = len(turned)
    tokens = sum(piece.shape[1] for piece in turned)

    def kernel(*refs):
        out_ref = refs[-1]
        left = jnp.concatenate([ref[...] for ref in refs[:count]], axis=1)
        right = jnp.concatenate([ref[...] for ref in refs[count : 2 * count]], axis=0)
        product = jnp.dot(left, right, preferred_element_type=F32)
        out_ref[...] = (product * scale).astype(BF)

    args = list(turned) + list(grads)
    specs = [pl.BlockSpec((size, piece.shape[1]), lambda i: (i, 0)) for piece in turned]
    specs += [pl.BlockSpec(piece.shape, lambda i: (0, 0)) for piece in grads]
    aliases = None
    if result is not None:
        args.append(result)
        specs.append(pl.BlockSpec(memory_space=pl.ANY))
        aliases = {2 * count: 0}
    return call(
        "weight_grad",
        kernel,
        (steps,),
        specs,
        pl.BlockSpec((size, columns), lambda i: (start + i, 0)),
        jax.ShapeDtypeStruct((total, columns), BF),
        2 * tokens * width * columns,
        2 * width * (columns + tokens),
        aliases=aliases,
    )(*args)


ORDER = [
    "h3", "G", "G", "h0", "h2", "G", "h2", "g3", "g0", "h0", "h1", "g1",
    "h2", "g3", "G", "g0", "g2", "h3", "g3", "h1", "h2", "G", "g2", "h3",
    "g1", "h2", "h3", "h0", "h3", "h1", "h2", "g3", "h1", "g0", "g1", "h0",
    "h1", "h0", "g2", "h1", "h2", "out", "g1", "h0", "g0", "h1", "h0", "h3",
    "g2", "out", "h3", "out",
]


def body(hidden, weight, out_grad):
    n_tensor, n_seq, n_dp = (lax.axis_size(a) for a in ("tensor", "seq", "dp"))
    me_tensor, me_seq = lax.axis_index("tensor"), lax.axis_index("seq")
    rows, features = hidden.shape
    blocks = features // HB
    per_seq = n_tensor // n_seq
    table = walsh_table(HB)
    norm_scale = 1.0 / float(n_tensor * HB) ** 0.5
    grad_scale = 1.0 / float(rows * n_seq * n_dp) ** 0.5
    signs = [sign_of("tensor", bit) for bit in range(bits_of("tensor"))]
    plus = jnp.ones((1, 1), F32)
    near_first = list(range(bits_of("tensor")))
    far_first = near_first[::-1]
    seq_bits = list(range(bits_of("seq")))
    dp_bits = list(reversed(range(bits_of("dp"))))
    hidden_parts = split_blocks(blocks, HIDDEN_SPLIT)
    grad_parts = split_blocks(blocks, GRAD_SPLIT)
    state = {"last": None, "running": None, "grad_weight": None, "grad_hidden": None}
    state["to_sum"] = len(hidden_parts)

    def tied(value):
        if state["last"] is None:
            return value
        return lax.optimization_barrier((value, state["last"]))[0]

    def done(value):
        state["last"] = value
        return value

    def send(value, axis, bit):
        return partner(tied(value), axis, bit)

    def gather_grads():
        grads = out_grad
        for bit in far_first:
            arrived = partner(grads, "tensor", bit)
            yield
            grads = done(jnp.concatenate([grads, arrived], axis=0))
        shards = grads.reshape(n_tensor, *out_grad.shape)

        def shard_of(owner):
            apart = owner ^ me_tensor
            place = sum(((apart >> b) & 1) << (len(near_first) - 1 - b) for b in near_first)
            return lax.dynamic_index_in_dim(shards, place, 0, keepdims=False)

        grads = done(
            jnp.concatenate(
                [
                    shard_of((me_seq ^ run) * per_seq + inner)
                    for run in range(n_seq)
                    for inner in range(per_seq)
                ],
                axis=0,
            )
        )
        state["grads"] = grads
        pieces = [grads]
        for bit in dp_bits:
            pieces += [send(piece, "dp", bit) for piece in pieces[::-1]][::-1]
            yield
            for piece in pieces[len(pieces) // 2 :]:
                done(piece)
        state["grad_pieces"] = pieces

    def hidden_part(first, size):
        sent = tied(hidden)[:, first * HB : (first + size) * HB]
        for bit in far_first[:-1]:
            arrived = send(sent, "tensor", bit)
            yield
            sent = done(combine(signs[bit], tied(sent), arrived))
        arrived = send(sent, "tensor", far_first[-1])
        yield
        turned = done(finish_hidden(signs[far_first[-1]], tied(sent), arrived, table, norm_scale))
        for bit in seq_bits:
            arrived = send(turned, "seq", bit)
            yield
            turned = done(jnp.concatenate([tied(turned), arrived], axis=1))
        pieces = [turned]
        for place, bit in enumerate(dp_bits):
            pieces += [send(piece, "dp", bit) for piece in pieces]
            yield
            if place == 0:
                state["to_sum"] -= 1
                state["running"] = done(
                    output_part(
                        tied(turned), weight, first, state["running"], state["to_sum"] == 0
                    )
                )
                yield
        state["grad_weight"] = done(
            weight_grad_part(
                [tied(pieces[0])] + pieces[1:],
                state["grad_pieces"],
                grad_scale,
                first,
                features,
                state["grad_weight"],
            )
        )

    def grad_part(first, size):
        terms = list(rotated_grad_parts(tied(state["grads"]), weight, first, size, n_seq))
        done(terms[0])
        for bit in reversed(seq_bits):
            half = len(terms) // 2
            arrived = [send(term, "seq", bit) for term in terms[half:]]
            yield
            terms = [
                done(combine(plus, tied(terms[n]), arrived[n])) for n in range(half)
            ]
        own = terms[0]
        for bit in near_first[:-1]:
            arrived = send(own, "tensor", bit)
            yield
            own = done(combine(signs[bit], tied(own), arrived))
        arrived = send(own, "tensor", near_first[-1])
        yield
        state["grad_hidden"] = done(
            finish_grad(
                signs[near_first[-1]],
                tied(own),
                arrived,
                table,
                norm_scale,
                first,
                features,
                state["grad_hidden"],
            )
        )

    def sum_output():
        shard_rows = out_grad.shape[0]
        runs = state["running"].reshape(n_tensor, shard_rows, -1)

        def run_for(apart):
            owner = me_tensor ^ apart
            place = ((owner // per_seq) ^ me_seq) * per_seq + owner % per_seq
            return lax.dynamic_index_in_dim(runs, place, 0, keepdims=False)

        sums = {apart: run_for(apart) for apart in range(n_tensor)}
        for bit in near_first:
            leaving = [apart for apart in sums if apart >> bit & 1]
            arrived = partner(jnp.concatenate([sums[a] for a in leaving], axis=0), "tensor", bit)
            yield
            arrived = tied(arrived)
            for place, apart in enumerate(leaving):
                block = arrived[place * shard_rows : (place + 1) * shard_rows]
                kept = apart ^ 1 << bit
                sums[kept] = (sums[kept].astype(F32) + block.astype(F32)).astype(BF)
                del sums[apart]
            done(sums[0])
        state["output"] = sums[0]

    steps = {"G": gather_grads()}
    for n, (first, size) in enumerate(hidden_parts):
        steps["h%d" % n] = hidden_part(first, size)
    for n, (first, size) in enumerate(grad_parts):
        steps["g%d" % n] = grad_part(first, size)
    steps["out"] = sum_output()
    order = ORDER
    if (n_tensor, n_seq, n_dp) != (4, 2, 4):
        order = ["G"] * 20
        for name in [n for n in steps if n[0] in "hg"]:
            order += [name] * 20
        order += ["out"] * 10
    for name in order:
        next(steps[name], None)
    return (state["output"], state["grad_hidden"], state["grad_weight"])


def solution(mesh):
    in_specs = (P(("dp", "seq"), "tensor"), P("tensor", "seq"), P(("dp", "tensor"), "seq"))
    out_specs = (P(("dp", "tensor"), "seq"), P(("dp", "seq"), "tensor"), P("tensor", "seq"))
    return jax.shard_map(body, mesh=mesh, in_specs=in_specs, out_specs=out_specs, check_vma=False)
```

```python
import functools

import jax
import jax.numpy as jnp
from jax import lax
from jax.experimental import pallas as pl
from jax.experimental.pallas import tpu as pltpu
from jax.sharding import PartitionSpec as P

HB = 512
BF = jnp.bfloat16
F32 = jnp.float32
VMEM_BYTES = 40 * 1024 * 1024
HIDDEN_SPLIT = (3, 3, 4, 4)
GRAD_SPLIT = (3, 3, 4, 4)
PLANNED = {'weight_grad': 0.01, 'combine': 0.01}
def partner(shard, axis, bit):
    return lax.ppermute(shard, axis, [(i, i ^ 1 << bit) for i in range(lax.axis_size(axis))])


def bits_of(axis):
    return lax.axis_size(axis).bit_length() - 1


def walsh_table(table_order):
    matrix = jnp.ones((1, 1), F32)
    while matrix.shape[0] < table_order:
        matrix = jnp.concatenate(
            [jnp.concatenate([matrix, matrix], 1), jnp.concatenate([matrix, -matrix], 1)], 0
        )
    return matrix.astype(BF)


def split_blocks(total, sizes):
    if sum(sizes) != total:
        count = min(len(sizes), total)
        sizes = [total // count + (1 if i < total % count else 0) for i in range(count)]
    return [(sum(sizes[:i]), sizes[i]) for i in range(len(sizes))]


def call(name, kernel, grid, in_specs, out_specs, out_shape, flops, nbytes, scratch=(), aliases=None):
    weight = PLANNED.get(name, 1)
    return pl.pallas_call(
        kernel,
        name=name,
        grid=grid,
        in_specs=in_specs,
        out_specs=out_specs,
        out_shape=out_shape,
        scratch_shapes=list(scratch),
        input_output_aliases=aliases or {},
        compiler_params=pltpu.CompilerParams(vmem_limit_bytes=VMEM_BYTES),
        cost_estimate=pl.CostEstimate(flops=int(flops * weight), bytes_accessed=int(nbytes * weight), transcendentals=0),
    )


def sign_of(axis, bit):
    upper = lax.rem(lax.div(lax.axis_index(axis), 1 << bit), 2)
    return (1 - 2 * upper).astype(F32).reshape(1, 1)


SIGN_SPEC = pl.BlockSpec(memory_space=pltpu.SMEM)


def steps_for(first, blocks, least, unit):
    for steps in range(least, blocks + 1):
        size = blocks * HB // steps
        if size * steps == blocks * HB and size % unit == 0 and first * HB % size == 0:
            return steps, size, first * HB // size
    return blocks, HB, first


def combine(sign, own, received):
    rows, width = received.shape

    def kernel(sign_ref, own_ref, received_ref, out_ref):
        out_ref[...] = (
            received_ref[...].astype(F32) + sign_ref[0, 0] * own_ref[...].astype(F32)
        ).astype(BF)

    whole = pl.BlockSpec((rows, width), lambda i: (0, 0))
    return call(
        "combine",
        kernel,
        (1,),
        [SIGN_SPEC, whole, whole],
        whole,
        jax.ShapeDtypeStruct((rows, width), BF),
        2 * rows * width,
        6 * rows * width,
    )(sign, own, received)


def finish_hidden(sign, own, received, table, scale):
    rows, width = received.shape

    def kernel(sign_ref, own_ref, received_ref, table_ref, out_ref):
        for at in range(0, width, HB):
            run = slice(at, at + HB)
            mixed = received_ref[:, run].astype(F32) + sign_ref[0, 0] * own_ref[:, run].astype(F32)
            turned = lax.dot_general(
                table_ref[...],
                mixed.astype(BF),
                (((1,), (1,)), ((), ())),
                preferred_element_type=F32,
            )
            out_ref[run, :] = (turned * scale).astype(BF)

    whole = pl.BlockSpec((rows, width), lambda i: (0, 0))
    return call(
        "finish_hidden",
        kernel,
        (1,),
        [SIGN_SPEC, whole, whole, pl.BlockSpec((HB, HB), lambda i: (0, 0))],
        pl.BlockSpec((width, rows), lambda i: (0, 0)),
        jax.ShapeDtypeStruct((width, rows), BF),
        2 * rows * width * HB,
        6 * rows * width,
    )(sign, own, received, table)


def finish_grad(sign, own, received, table, scale, first, total, result):
    rows, width = received.shape
    steps, size, start = steps_for(first, width // HB, 1, HB)

    def kernel(sign_ref, own_ref, received_ref, table_ref, *refs):
        out_ref = refs[-1]
        for at in range(0, size, HB):
            run = slice(at, at + HB)
            mixed = received_ref[:, run].astype(F32) + sign_ref[0, 0] * own_ref[:, run].astype(F32)
            turned = jnp.dot(mixed.astype(BF), table_ref[...], preferred_element_type=F32)
            out_ref[:, run] = (turned * scale).astype(BF)

    args = [sign, own, received, table]
    specs = [
        SIGN_SPEC,
        pl.BlockSpec((rows, size), lambda i: (0, i)),
        pl.BlockSpec((rows, size), lambda i: (0, i)),
        pl.BlockSpec((HB, HB), lambda i: (0, 0)),
    ]
    aliases = None
    if result is not None:
        args.append(result)
        specs.append(pl.BlockSpec(memory_space=pl.ANY))
        aliases = {4: 0}
    return call(
        "finish_grad",
        kernel,
        (steps,),
        specs,
        pl.BlockSpec((rows, size), lambda i: (0, start + i)),
        jax.ShapeDtypeStruct((rows, total), BF),
        2 * rows * width * HB,
        6 * rows * width,
        aliases=aliases,
    )(*args)


def rotated_grad_parts(grads, weight, first, blocks, count):
    tokens, columns = grads.shape
    rows = tokens // count
    steps, size, start = steps_for(first, blocks, 2, 256)

    def kernel(grads_ref, weight_ref, *out_refs):
        total = lax.dot_general(
            grads_ref[...], weight_ref[...], (((1,), (1,)), ((), ())), preferred_element_type=F32
        ).astype(BF)
        for n, out_ref in enumerate(out_refs):
            out_ref[...] = total[n * rows : (n + 1) * rows]

    return call(
        "rotated_grad",
        kernel,
        (steps,),
        [
            pl.BlockSpec((tokens, columns), lambda i: (0, 0)),
            pl.BlockSpec((size, columns), lambda i: (start + i, 0)),
        ],
        [pl.BlockSpec((rows, size), lambda i: (0, i))] * count,
        [jax.ShapeDtypeStruct((rows, blocks * HB), BF)] * count,
        2 * tokens * columns * blocks * HB,
        2 * blocks * HB * columns,
    )(grads, weight)


def output_part(turned, weight, first, running, last):
    width, tokens = turned.shape
    columns = weight.shape[1]
    steps, size, start = steps_for(first, width // HB, 2, 256)

    def kernel(turned_ref, weight_ref, *refs):
        total_ref = refs[-1]
        out_ref = refs[-2]
        step = pl.program_id(0)

        @pl.when(step == 0)
        def _():
            if running is None:
                total_ref[...] = jnp.zeros_like(total_ref)
            else:
                total_ref[...] = refs[0][...]

        total_ref[...] += lax.dot_general(
            turned_ref[...], weight_ref[...], (((0,), (0,)), ((), ())), preferred_element_type=F32
        )

        @pl.when(step == steps - 1)
        def _():
            out_ref[...] = total_ref[...].astype(out_ref.dtype)

    whole = pl.BlockSpec((tokens, columns), lambda i: (0, 0))
    args = [turned, weight]
    specs = [
        pl.BlockSpec((size, tokens), lambda i: (i, 0)),
        pl.BlockSpec((size, columns), lambda i: (start + i, 0)),
    ]
    if running is not None:
        args.append(running)
        specs.append(whole)
    return call(
        "output",
        kernel,
        (steps,),
        specs,
        whole,
        jax.ShapeDtypeStruct((tokens, columns), BF if last else F32),
        2 * tokens * width * columns,
        2 * width * columns,
        scratch=[pltpu.VMEM((tokens, columns), F32)],
    )(*args)


def weight_grad_part(turned, grads, scale, first, total, result):
    width = turned[0].shape[0]
    columns = grads[0].shape[1]
    steps, size, start = steps_for(first, width // HB, width // HB, 256)
    count = len(turned)
    tokens = sum(piece.shape[1] for piece in turned)

    def kernel(*refs):
        out_ref = refs[-1]
        left = jnp.concatenate([ref[...] for ref in refs[:count]], axis=1)
        right = jnp.concatenate([ref[...] for ref in refs[count : 2 * count]], axis=0)
        product = jnp.dot(left, right, preferred_element_type=F32)
        out_ref[...] = (product * scale).astype(BF)

    args = list(turned) + list(grads)
    specs = [pl.BlockSpec((size, piece.shape[1]), lambda i: (i, 0)) for piece in turned]
    specs += [pl.BlockSpec(piece.shape, lambda i: (0, 0)) for piece in grads]
    aliases = None
    if result is not None:
        args.append(result)
        specs.append(pl.BlockSpec(memory_space=pl.ANY))
        aliases = {2 * count: 0}
    return call(
        "weight_grad",
        kernel,
        (steps,),
        specs,
        pl.BlockSpec((size, columns), lambda i: (start + i, 0)),
        jax.ShapeDtypeStruct((total, columns), BF),
        2 * tokens * width * columns,
        2 * width * (columns + tokens),
        aliases=aliases,
    )(*args)


ORDER = [
    "h3", "G", "G", "h0", "h2", "G", "h2", "g3", "g0", "h0", "h1", "g1",
    "h2", "g3", "G", "g0", "g2", "h3", "g3", "h1", "h2", "G", "g2", "h3",
    "g1", "h2", "h3", "h0", "h3", "h1", "h2", "g3", "h1", "g0", "g1", "h0",
    "h1", "h0", "g2", "h1", "h2", "out", "g1", "h0", "g0", "h1", "h0", "h3",
    "g2", "out", "h3", "out",
]


def body(hidden, weight, out_grad):
    n_tensor, n_seq, n_dp = (lax.axis_size(a) for a in ("tensor", "seq", "dp"))
    me_tensor, me_seq = lax.axis_index("tensor"), lax.axis_index("seq")
    rows, features = hidden.shape
    blocks = features // HB
    per_seq = n_tensor // n_seq
    table = walsh_table(HB)
    norm_scale = 1.0 / float(n_tensor * HB) ** 0.5
    grad_scale = 1.0 / float(rows * n_seq * n_dp) ** 0.5
    signs = [sign_of("tensor", bit) for bit in range(bits_of("tensor"))]
    plus = jnp.ones((1, 1), F32)
    near_first = list(range(bits_of("tensor")))
    far_first = near_first[::-1]
    seq_bits = list(range(bits_of("seq")))
    dp_bits = list(reversed(range(bits_of("dp"))))
    hidden_parts = split_blocks(blocks, HIDDEN_SPLIT)
    grad_parts = split_blocks(blocks, GRAD_SPLIT)
    state = {"last": None, "running": None, "grad_weight": None, "grad_hidden": None}
    state["to_sum"] = len(hidden_parts)

    def tied(value):
        if state["last"] is None:
            return value
        return lax.optimization_barrier((value, state["last"]))[0]

    def done(value):
        state["last"] = value
        return value

    def send(value, axis, bit):
        return partner(tied(value), axis, bit)

    def gather_grads():
        grads = out_grad
        for bit in far_first:
            arrived = partner(grads, "tensor", bit)
            yield
            grads = done(jnp.concatenate([grads, arrived], axis=0))
        shards = grads.reshape(n_tensor, *out_grad.shape)

        def shard_of(owner):
            apart = owner ^ me_tensor
            place = sum(((apart >> b) & 1) << (len(near_first) - 1 - b) for b in near_first)
            return lax.dynamic_index_in_dim(shards, place, 0, keepdims=False)

        grads = done(
            jnp.concatenate(
                [
                    shard_of((me_seq ^ run) * per_seq + inner)
                    for run in range(n_seq)
                    for inner in range(per_seq)
                ],
                axis=0,
            )
        )
        state["grads"] = grads
        pieces = [grads]
        for bit in dp_bits:
            pieces += [send(piece, "dp", bit) for piece in pieces[::-1]][::-1]
            yield
            for piece in pieces[len(pieces) // 2 :]:
                done(piece)
        state["grad_pieces"] = pieces

    def hidden_part(first, size):
        sent = tied(hidden)[:, first * HB : (first + size) * HB]
        for bit in far_first[:-1]:
            arrived = send(sent, "tensor", bit)
            yield
            sent = done(combine(signs[bit], tied(sent), arrived))
        arrived = send(sent, "tensor", far_first[-1])
        yield
        turned = done(finish_hidden(signs[far_first[-1]], tied(sent), arrived, table, norm_scale))
        for bit in seq_bits:
            arrived = send(turned, "seq", bit)
            yield
            turned = done(jnp.concatenate([tied(turned), arrived], axis=1))
        pieces = [turned]
        for place, bit in enumerate(dp_bits):
            pieces += [send(piece, "dp", bit) for piece in pieces]
            yield
            if place == 0:
                state["to_sum"] -= 1
                state["running"] = done(
                    output_part(
                        tied(turned), weight, first, state["running"], state["to_sum"] == 0
                    )
                )
                yield
        state["grad_weight"] = done(
            weight_grad_part(
                [tied(pieces[0])] + pieces[1:],
                state["grad_pieces"],
                grad_scale,
                first,
                features,
                state["grad_weight"],
            )
        )

    def grad_part(first, size):
        terms = list(rotated_grad_parts(tied(state["grads"]), weight, first, size, n_seq))
        done(terms[0])
        for bit in reversed(seq_bits):
            half = len(terms) // 2
            arrived = [send(term, "seq", bit) for term in terms[half:]]
            yield
            terms = [
                done(combine(plus, tied(terms[n]), arrived[n])) for n in range(half)
            ]
        own = terms[0]
        for bit in near_first[:-1]:
            arrived = send(own, "tensor", bit)
            yield
            own = done(combine(signs[bit], tied(own), arrived))
        arrived = send(own, "tensor", near_first[-1])
        yield
        state["grad_hidden"] = done(
            finish_grad(
                signs[near_first[-1]],
                tied(own),
                arrived,
                table,
                norm_scale,
                first,
                features,
                state["grad_hidden"],
            )
        )

    def sum_output():
        shard_rows = out_grad.shape[0]
        runs = state["running"].reshape(n_tensor, shard_rows, -1)

        def run_for(apart):
            owner = me_tensor ^ apart
            place = ((owner // per_seq) ^ me_seq) * per_seq + owner % per_seq
            return lax.dynamic_index_in_dim(runs, place, 0, keepdims=False)

        sums = {apart: run_for(apart) for apart in range(n_tensor)}
        for bit in near_first:
            leaving = [apart for apart in sums if apart >> bit & 1]
            arrived = partner(jnp.concatenate([sums[a] for a in leaving], axis=0), "tensor", bit)
            yield
            arrived = tied(arrived)
            for place, apart in enumerate(leaving):
                block = arrived[place * shard_rows : (place + 1) * shard_rows]
                kept = apart ^ 1 << bit
                sums[kept] = (sums[kept].astype(F32) + block.astype(F32)).astype(BF)
                del sums[apart]
            done(sums[0])
        state["output"] = sums[0]

    steps = {"G": gather_grads()}
    for n, (first, size) in enumerate(hidden_parts):
        steps["h%d" % n] = hidden_part(first, size)
    for n, (first, size) in enumerate(grad_parts):
        steps["g%d" % n] = grad_part(first, size)
    steps["out"] = sum_output()
    order = ORDER
    if (n_tensor, n_seq, n_dp) != (4, 2, 4):
        order = ["G"] * 20
        for name in [n for n in steps if n[0] in "hg"]:
            order += [name] * 20
        order += ["out"] * 10
    for name in order:
        next(steps[name], None)
    return (state["output"], state["grad_hidden"], state["grad_weight"])


def solution(mesh):
    in_specs = (P(("dp", "seq"), "tensor"), P("tensor", "seq"), P(("dp", "tensor"), "seq"))
    out_specs = (P(("dp", "tensor"), "seq"), P(("dp", "seq"), "tensor"), P("tensor", "seq"))
    return jax.shard_map(body, mesh=mesh, in_specs=in_specs, out_specs=out_specs, check_vma=False)
```
